32 devices in a mesh: grp: 2 (over x), feat: 16 (over z, y, core).
Axes of the slice: x: 2, y: 2, z: 4, core: 2. Of those that a mesh axis runs over, the one named last changes fastest.
Arguments:
- node_feats: bfloat16 [65536, 128], P(('grp', 'feat')), parts along dimension 0, may hold values from -6 to 6
- tile_weights: bfloat16 [1024, 128, 128], P(('grp', 'feat')), parts along dimension 0, may hold values from 0 to 1
- source_slots: int32 [1024], P(('grp', 'feat')), parts along dimension 0, may hold values from 0 to 16, as said below
- target_slots: int32 [1024], P(('grp', 'feat')), parts along dimension 0, may hold values from 0 to 16, as said below
- self_weight: bfloat16 [128, 1024], replicated, may hold values from -0.5 to 0.5
- neigh_weight: bfloat16 [128, 1024], replicated, may hold values from -0.5 to 0.5
- hidden_bias: float32 [1024], replicated, may hold values from -3 to 3
- out_grad: bfloat16 [65536, 1024], P(('grp', 'feat')), parts along dimension 0, may hold values from -6 to 6
Outputs:
- feat_grad: bfloat16 [65536, 128], P(('grp', 'feat')), parts along dimension 0
- self_grad: float32 [256, 1024], P('grp', 'feat'), parts along dimension 0
- neigh_grad: float32 [256, 1024], P('grp', 'feat'), parts along dimension 0
- bias_grad: float32 [2048], P(('grp', 'feat')), parts along dimension 0
The draws below stay inside these ranges and needn't reach their ends.
There are 2 independent parts, one for each index of `grp`. The reference program is written for one: setup_inputs(seed, part) draws one part's arguments, and reference() takes and returns one part's arrays. A program takes and returns all parts, laid end to end along the dimension named above; an argument that names none is the same for every part. Nothing has to cross between parts.
Inputs may be any that keep to these rules, and one draw needn't show every extreme that they name: `source_slots`: entry (s, r, k) is empty (16) exactly when target_slots entry (r, s, k) is empty. Filled slots of one pair of owners are uneven across owners; some owner receives 2 tiles from every owner. `target_slots`: empty entries (16) match those of source_slots as stated there.
All inputs are finite; a program needn't handle non-finite values.
Results may differ from the reference program's by a relative error of at most 0.0085.
The reference program's roundings to bfloat16 on the way (of `products`, `neigh_mean`, `pre_grad` and `mean_grad`) count: a program that leaves them out, or rounds other values in their place, can miss the bound.
Values may be sent and summed in bfloat16 or wider, within the bound.
A program may use at most 128 MiB of HBM per device.

```python
import jax
import jax.numpy as jnp
from jax import lax

FEATS = 128
HIDDEN_SIZE = 1024
TILE = 128
CAPACITY = 2
NODE_DEV = 2048
NODES = 32768
N_FEAT = 16


def slot_tables(key):
    blocks_dev = NODE_DEV // TILE
    keys = jax.random.split(key, 6)
    send_level = jax.random.randint(keys[0], (N_FEAT,), 1, 9)
    recv_level = jax.random.randint(keys[1], (N_FEAT,), 1, 9)
    rolls = jax.random.randint(keys[2], (N_FEAT, N_FEAT, CAPACITY), 0, 64)
    chosen = jax.random.randint(keys[3], (), 0, N_FEAT)
    owner_ids = jnp.arange(N_FEAT, dtype=jnp.int32)
    filled = (rolls < send_level[:, None, None] * recv_level[None, :, None]) | (owner_ids[None, :, None] == chosen)
    source_ids = jax.random.randint(keys[4], (N_FEAT, N_FEAT, CAPACITY), 0, blocks_dev)
    target_ids = jax.random.randint(keys[5], (N_FEAT, N_FEAT, CAPACITY), 0, blocks_dev)
    empty_id = jnp.full((N_FEAT, N_FEAT, CAPACITY), blocks_dev, dtype=jnp.int32)
    sources = jnp.where(filled, source_ids, empty_id)
    targets = jnp.where(filled, target_ids, empty_id)
    return (sources, targets)


def draw_source_slots(key, part):
    sources, targets = slot_tables(key)
    return sources.reshape(-1).astype(jnp.int32)


def draw_target_slots(key, part):
    sources, targets = slot_tables(key)
    return jnp.transpose(targets, (1, 0, 2)).reshape(-1).astype(jnp.int32)


def draw_tile_weights(key, part):
    sources, targets = slot_tables(key)
    key = jax.random.fold_in(key, 3)
    blocks_dev = NODE_DEV // TILE
    sampled = (jax.random.randint(key, (N_FEAT, N_FEAT, CAPACITY, TILE, TILE), 0, TILE) < 6).astype(jnp.int32)
    row_edges = jnp.sum(sampled, axis=-1)
    dest_owner = jnp.broadcast_to(jnp.arange(N_FEAT, dtype=jnp.int32)[None, :, None], (N_FEAT, N_FEAT, CAPACITY))
    degree = jnp.zeros((N_FEAT, blocks_dev + 1, TILE), jnp.int32).at[dest_owner, targets].add(row_edges)
    node_degree = jnp.maximum(degree[dest_owner, targets], 1).astype(jnp.float32)
    weights = sampled.astype(jnp.float32) / node_degree[..., None]
    return weights.reshape(N_FEAT * N_FEAT * CAPACITY, TILE, TILE).astype(jnp.bfloat16)


def spiked(result, stream_key, source, target, parts, factor):
    def block_of(dim):
        return (jnp.arange(result.shape[dim]) // (result.shape[dim] // parts)).reshape((-1,) + (1,) * (result.ndim - 1 - dim))

    first = jax.random.permutation(stream_key, parts)[block_of(target)]
    far = (block_of(target) + parts // 2) % parts
    return jnp.where((block_of(source) == first) | (block_of(source) == far), factor * result, result)


def levels(own_key, extent, shards, low, largest):
    def one(position, parts):
        draws = jax.random.uniform(jax.random.fold_in(jax.random.fold_in(own_key, 6), position), (parts,), jnp.float32, low / len(shards), largest / len(shards))
        return jnp.repeat(jnp.exp(draws), extent[position] // parts).reshape((-1,) + (1,) * (len(extent) - position - 1))

    gain = one(*shards[0])
    for cut in shards[1:]:
        gain = gain * one(*cut)
    return gain


def gaussian(key, shape, deviation, most, pieces=(), held_as=jnp.bfloat16):
    values = jax.random.normal(key, shape, jnp.float32) * deviation
    if len(pieces) > 0:
        values = levels(key, shape, pieces, -0.22, 0.18) * values
    return jnp.clip(values, min=-most, max=most).astype(held_as)


def gaussian_with(stream_key, shape, scale, reach, pieces, heavy, kind=jnp.bfloat16):
    values = scale * jax.random.normal(stream_key, shape, jnp.float32)
    if pieces:
        values = values * levels(stream_key, shape, pieces, -0.22, 0.18)
    return jnp.clip(spiked(values, jax.random.fold_in(stream_key, 3), *heavy), -reach, reach).astype(kind)


def setup_inputs(seed: int = 0, part: int = 0) -> dict:
    streams_of = jax.random.split(jax.random.key(seed), 9)
    part_splits = jax.random.split(jax.random.fold_in(streams_of[8], part), 9)
    return {
        "node_feats": gaussian(part_splits[0], (NODES, FEATS), 1.0, 6.0, ((0, 16),)),
        "tile_weights": draw_tile_weights(jax.random.fold_in(jax.random.fold_in(streams_of[8], part), 71), part),
        "source_slots": draw_source_slots(jax.random.fold_in(jax.random.fold_in(streams_of[8], part), 71), part),
        "target_slots": draw_target_slots(jax.random.fold_in(jax.random.fold_in(streams_of[8], part), 71), part),
        "self_weight": gaussian(streams_of[4], (FEATS, HIDDEN_SIZE), FEATS ** -0.5, 0.5),
        "neigh_weight": gaussian(streams_of[5], (FEATS, HIDDEN_SIZE), FEATS ** -0.5, 0.5),
        "hidden_bias": gaussian(streams_of[6], (HIDDEN_SIZE,), 0.5, 3.0, (), jnp.float32),
        "out_grad": gaussian_with(part_splits[7], (NODES, HIDDEN_SIZE), 1.0, 6.0, ((0, 16),), (0, 1, 16, 2.0)),
    }


def normalize(active):
    return active * lax.rsqrt(lax.optimization_barrier(jnp.mean(active * active, axis=-1, keepdims=True)) + 1e-05)

def reference(node_feats, tile_weights, source_slots, target_slots, self_weight, neigh_weight, hidden_bias, out_grad):
    blocks_dev = NODE_DEV // TILE
    highest = lax.Precision.HIGHEST
    owner_blocks = node_feats.reshape(N_FEAT, blocks_dev, TILE, FEATS)
    sources = source_slots.reshape(N_FEAT, N_FEAT, CAPACITY)
    filled = sources < blocks_dev
    clipped = jnp.minimum(sources, blocks_dev - 1).astype(jnp.int32)
    owners = jnp.arange(N_FEAT, dtype=jnp.int32)[:, None, None]
    picked = owner_blocks[owners, clipped].astype(jnp.float32)
    tile_mats = tile_weights.reshape(N_FEAT, N_FEAT, CAPACITY, TILE, TILE).astype(jnp.float32)
    products = jnp.einsum('srkij,srkjc->srkic', tile_mats, picked, precision=highest)
    products = jnp.where(filled[..., None, None], products, 0.0).astype(jnp.bfloat16)
    targets = target_slots.reshape(N_FEAT, N_FEAT, CAPACITY)
    block_ids = jnp.arange(blocks_dev, dtype=jnp.int32)
    onehot = (targets[..., None] == block_ids).astype(jnp.float32)
    incoming = jnp.transpose(products, (1, 0, 2, 3, 4)).astype(jnp.float32)
    summed = jnp.einsum('rskb,rskic->rbic', onehot, incoming, precision=highest)
    neigh_mean = summed.astype(jnp.bfloat16).reshape(N_FEAT * NODE_DEV, FEATS)
    preact = jnp.dot(node_feats, self_weight, preferred_element_type=jnp.float32) + jnp.dot(neigh_mean, neigh_weight, preferred_element_type=jnp.float32) + hidden_bias
    active = jnp.maximum(preact, 0.0)
    output_value, pullback = jax.vjp(normalize, active)
    active_grad = pullback(out_grad.astype(jnp.float32))[0]
    pre_grad = jnp.where(preact > 0.0, active_grad, 0.0).astype(jnp.bfloat16)
    bias_grad = lax.optimization_barrier(jnp.sum(pre_grad.astype(jnp.float32), axis=0))
    self_grad = jnp.dot(node_feats.T, pre_grad, preferred_element_type=jnp.float32)
    neigh_grad = jnp.dot(neigh_mean.T, pre_grad, preferred_element_type=jnp.float32)
    mean_grad = jnp.dot(pre_grad, neigh_weight.T, preferred_element_type=jnp.float32)
    mean_grad = mean_grad.astype(jnp.bfloat16).astype(jnp.float32).reshape(N_FEAT, blocks_dev, TILE, FEATS)
    returned = jnp.einsum('rskb,rbic->rskic', onehot, mean_grad, precision=highest)
    returned = jnp.transpose(returned, (1, 0, 2, 3, 4))
    spread = jnp.einsum('srkji,srkjc->srkic', tile_mats, returned, precision=highest)
    source_hot = (sources[..., None] == block_ids).astype(jnp.float32)
    gathered_back = jnp.einsum('srkb,srkic->sbic', source_hot, spread, precision=highest)
    feat_grad = (jnp.dot(pre_grad, self_weight.T, preferred_element_type=jnp.float32) + gathered_back.reshape(N_FEAT * NODE_DEV, FEATS)).astype(jnp.bfloat16)
    return (feat_grad, self_grad, neigh_grad, bias_grad)
```

```python
import functools

import jax
import jax.numpy as jnp
from jax import lax
from jax.experimental import pallas as pl
from jax.experimental.pallas import tpu as pltpu
from jax.sharding import PartitionSpec as P

FEATS = 128
HIDDEN_SIZE = 1024
TILE = 128
CAPACITY = 2
NODE_DEV = 2048
BLOCKS = NODE_DEV // TILE
ROWS = 256
COLS = 256
BIAS_ROWS = 16
EARLY = 3
MESH = pl.DeviceIdType.MESH
F32 = jnp.float32
BF16 = jnp.bfloat16


def distance(step, n):
    q = jnp.maximum(step - 1, 0)
    far = n // 2 + ((q + 1) // 2) * (1 - 2 * (q % 2))
    return far * jnp.minimum(step, 1)


def split_bias(total):
    high = total.astype(BF16)
    low = (total - high.astype(F32)).astype(BF16)
    row = lax.broadcasted_iota(jnp.int32, (BIAS_ROWS, total.shape[1]), 0)
    both = jnp.where(row == 0, high.astype(F32), jnp.where(row == 1, low.astype(F32), 0.0))
    return both.astype(BF16)


def kernel(
    n,
    feats,
    tiles,
    source,
    target,
    self_w,
    neigh_w,
    bias,
    grad_hbm,
    feat_out,
    self_out,
    neigh_out,
    bias_out,
    grad,
    stage,
    arrived,
    back_stage,
    back,
    chain,
    weights,
    inputs,
    active,
    pre_grad,
    mean_grad,
    feat_self,
    weight_sum,
    bias_sum,
    pair_send,
    pair_recv,
    share_send,
    share_recv,
    swap_send,
    swap_recv,
    prev_t,
    last_t,
    prev_s,
    last_s,
    grad_sem,
    send_1,
    recv_1,
    send_2,
    recv_2,
    pair_sems,
    send_b,
    recv_b,
    swap_sems,
):
    chips = n // 2
    width = 2 * HIDDEN_SIZE // n
    half = width // 2
    slots = n * CAPACITY
    me = lax.axis_index("feat")
    core = me % 2
    chip = me // 2
    sibling = chip * 2 + 1 - core

    barrier = pltpu.get_barrier_semaphore()

    @pl.loop(1, n)
    def _(d):
        pl.semaphore_signal(
            barrier, inc=1, device_id={"feat": (me + d) % n}, device_id_type=MESH
        )

    grad_copy = pltpu.make_async_copy(grad_hbm, grad, grad_sem)
    grad_copy.start()

    def product(slot):
        block = feats[jnp.minimum(source[slot], BLOCKS - 1)]
        return jnp.dot(tiles[slot], block, preferred_element_type=F32).astype(BF16)

    def forward_copy(step):
        to = (me + distance(step, n)) % n
        return pltpu.make_async_remote_copy(
            src_ref=stage.at[to],
            dst_ref=arrived.at[me],
            send_sem=send_1.at[to],
            recv_sem=recv_1.at[me],
            device_id={"feat": to},
            device_id_type=MESH,
        )

    def forward_products(step):
        to = (me + distance(step, n)) % n
        for k in range(CAPACITY):
            stage[to, k] = product(to * CAPACITY + k)

    @pl.loop(1, 1 + EARLY)
    def _(step):
        forward_products(step)

    pl.semaphore_wait(barrier, n - 1)

    @pl.loop(1, 1 + EARLY)
    def _(step):
        forward_copy(step).start()

    @pl.loop(1 + EARLY, n)
    def _(step):
        forward_products(step)
        forward_copy(step).start()

    for k in range(CAPACITY):
        arrived[me, k] = product(me * CAPACITY + k)
    weights[:FEATS] = self_w[...]
    weights[FEATS:] = neigh_w[...]
    for b in range(BLOCKS):
        inputs[b * TILE : (b + 1) * TILE, :FEATS] = feats[b]
    chain[slots] = jnp.zeros((TILE, FEATS), F32)
    bias_sum[...] = jnp.zeros_like(bias_sum)

    for prev, last, table in ((prev_t, last_t, target), (prev_s, last_s, source)):
        for b in range(BLOCKS + 1):
            last[b] = slots

        @pl.loop(0, n)
        def _(step):
            owner = (me - distance(step, n) + n) % n
            for k in range(CAPACITY):
                at = step * CAPACITY + k
                block = table[owner * CAPACITY + k]
                prev[at] = last[block]
                for b in range(BLOCKS + 1):
                    last[b] = jnp.where(block == b, at, last[b])

    def forward_link(step, owner):
        for k in range(CAPACITY):
            at = step * CAPACITY + k
            chain[at] = arrived[owner, k].astype(F32) + chain[prev_t[at]]

    forward_link(0, me)

    @pl.loop(1, n)
    def _(step):
        owner = (me - distance(step, n) + n) % n
        pltpu.make_async_remote_copy(
            src_ref=stage.at[owner],
            dst_ref=arrived.at[owner],
            send_sem=send_1.at[owner],
            recv_sem=recv_1.at[owner],
            device_id={"feat": owner},
            device_id_type=MESH,
        ).wait_recv()
        forward_link(step, owner)

    for b in range(BLOCKS):
        inputs[b * TILE : (b + 1) * TILE, FEATS:] = chain[last_t[b]].astype(BF16)
    grad_copy.wait()

    @pl.loop(0, NODE_DEV // ROWS)
    def _(part):
        rows = pl.ds(pl.multiple_of(part * ROWS, ROWS), ROWS)
        x = inputs[rows, :]
        squares = jnp.zeros((ROWS, 128), F32)
        crosses = jnp.zeros((ROWS, 128), F32)
        for c in range(0, HIDDEN_SIZE, COLS):
            cols = slice(c, c + COLS)
            pre = jnp.dot(x, weights[:, cols], preferred_element_type=F32) + bias[:, cols]
            a = jnp.maximum(pre, 0.0)
            active[:, cols] = a
            g = grad[rows, cols].astype(F32)
            aa = a * a
            ag = a * g
            for e in range(0, COLS, 128):
                squares += aa[:, e : e + 128]
                crosses += ag[:, e : e + 128]
        scale = lax.rsqrt(jnp.sum(squares, axis=1, keepdims=True) / HIDDEN_SIZE + 1e-05)
        pull = scale * scale * scale * (jnp.sum(crosses, axis=1, keepdims=True) / HIDDEN_SIZE)
        for c in range(0, HIDDEN_SIZE, COLS):
            cols = slice(c, c + COLS)
            a = active[:, cols]
            g = grad[rows, cols].astype(F32)
            p = jnp.where(a > 0.0, scale * g - pull * a, 0.0).astype(BF16)
            pre_grad[rows, cols] = p
            bias_sum[:, cols] += jnp.sum(p.astype(F32).reshape(ROWS // 8, 8, COLS), axis=0)
        both = lax.dot_general(
            pre_grad[rows, :],
            weights[...],
            (((1,), (1,)), ((), ())),
            preferred_element_type=F32,
        )
        for e in range(ROWS // TILE):
            b = part * (ROWS // TILE) + e
            feat_self[b] = both[e * TILE : (e + 1) * TILE, :FEATS]
            mean_grad[b] = both[e * TILE : (e + 1) * TILE, FEATS:].astype(BF16)

    def backward_copy(step):
        to = (me + distance(step, n)) % n
        return pltpu.make_async_remote_copy(
            src_ref=back_stage.at[to],
            dst_ref=back.at[me],
            send_sem=send_2.at[to],
            recv_sem=recv_2.at[me],
            device_id={"feat": to},
            device_id_type=MESH,
        )

    def backward_send(step):
        to = (me + distance(step, n)) % n
        for k in range(CAPACITY):
            block = jnp.minimum(target[to * CAPACITY + k], BLOCKS - 1)
            back_stage[to, k] = mean_grad[block]
        backward_copy(step).start()

    @pl.loop(1, 1 + n // 2)
    def _(step):
        backward_send(step)

    for c in range(0, HIDDEN_SIZE, COLS):
        cols = slice(c, c + COLS)
        local = lax.dot_general(
            inputs[...],
            pre_grad[:, cols],
            (((0,), (0,)), ((), ())),
            preferred_element_type=F32,
        )
        weight_sum[0, :, cols] = local[:FEATS]
        weight_sum[1, :, cols] = local[FEATS:]
    bias_row = jnp.sum(bias_sum[...], axis=0, keepdims=True)
    for c in range(chips):
        cols = slice(c * width, (c + 1) * width)
        pair_send[c, :FEATS] = weight_sum[1 - core, :, cols].astype(BF16)
        pair_send[c, FEATS:] = split_bias(bias_row[:, cols])
    pair_copy = pltpu.make_async_remote_copy(
        src_ref=pair_send,
        dst_ref=pair_recv,
        send_sem=pair_sems.at[0],
        recv_sem=pair_sems.at[1],
        device_id={"feat": sibling},
        device_id_type=MESH,
    )
    pair_copy.start()
    pair_copy.wait_recv()
    for c in range(chips):
        cols = slice(c * width, (c + 1) * width)
        share_send[c, :FEATS] = (
            weight_sum[core, :, cols] + pair_recv[c, :FEATS].astype(F32)
        ).astype(BF16)
        other = jnp.sum(pair_recv[c, FEATS:].astype(F32), axis=0, keepdims=True)
        share_send[c, FEATS:] = split_bias(bias_row[:, cols] + other)

    def share_copy(to, slot):
        return pltpu.make_async_remote_copy(
            src_ref=share_send.at[to],
            dst_ref=share_recv.at[slot],
            send_sem=send_b.at[to],
            recv_sem=recv_b.at[slot],
            device_id={"feat": to * 2 + core},
            device_id_type=MESH,
        )

    @pl.loop(1, chips)
    def _(d):
        share_copy((chip + d) % chips, chip).start()

    @pl.loop(1 + n // 2, n)
    def _(step):
        backward_send(step)

    def backward_link(step, owner, blocks):
        for k in range(CAPACITY):
            at = step * CAPACITY + k
            spread = lax.dot_general(
                tiles[owner * CAPACITY + k],
                blocks[k],
                (((0,), (0,)), ((), ())),
                preferred_element_type=F32,
            )
            chain[at] = spread + chain[prev_s[at]]

    backward_link(
        0,
        me,
        [
            mean_grad[jnp.minimum(target[me * CAPACITY + k], BLOCKS - 1)]
            for k in range(CAPACITY)
        ],
    )

    def backward_take(step):
        owner = (me - distance(step, n) + n) % n
        pltpu.make_async_remote_copy(
            src_ref=back_stage.at[owner],
            dst_ref=back.at[owner],
            send_sem=send_2.at[owner],
            recv_sem=recv_2.at[owner],
            device_id={"feat": owner},
            device_id_type=MESH,
        ).wait_recv()
        backward_link(step, owner, [back[owner, k] for k in range(CAPACITY)])

    @pl.loop(1, 1 + n // 2)
    def _(step):
        backward_take(step)

    swap_send[...] = share_send[chip].astype(F32)

    @pl.loop(1, chips)
    def _(d):
        other = (chip + d) % chips
        share_copy(other, other).wait_recv()
        swap_send[...] += share_recv[other].astype(F32)

    swap_copy = pltpu.make_async_remote_copy(
        src_ref=swap_send,
        dst_ref=swap_recv,
        send_sem=swap_sems.at[0],
        recv_sem=swap_sems.at[1],
        device_id={"feat": sibling},
        device_id_type=MESH,
    )
    swap_copy.start()

    @pl.loop(1 + n // 2, n)
    def _(step):
        backward_take(step)

    for b in range(BLOCKS):
        feat_out[b] = (feat_self[b] + chain[last_s[b]]).astype(BF16)

    swap_copy.wait_recv()

    def own_half(block):
        return jnp.where(core == 0, block[:, :half], block[:, half:])

    mine = own_half(swap_send[:FEATS])
    theirs = own_half(swap_recv[:FEATS])
    self_out[...] = jnp.where(core == 0, mine, theirs)
    neigh_out[...] = jnp.where(core == 0, theirs, mine)
    bias_out[...] = own_half(jnp.sum(swap_send[FEATS:], axis=0, keepdims=True))

    swap_copy.wait_send()
    pair_copy.wait_send()

    @pl.loop(1, chips)
    def _(d):
        share_copy((chip + d) % chips, chip).wait_send()

    @pl.loop(1, n)
    def _(step):
        forward_copy(step).wait_send()
        backward_copy(step).wait_send()


def local(
    node_feats,
    tile_weights,
    source_slots,
    target_slots,
    self_weight,
    neigh_weight,
    hidden_bias,
    out_grad,
):
    n = lax.axis_size("feat")
    slots = n * CAPACITY
    chips = n // 2
    width = 2 * HIDDEN_SIZE // n
    share_rows = FEATS + BIAS_ROWS
    vmem = pl.BlockSpec(memory_space=pltpu.VMEM)
    smem = pl.BlockSpec(memory_space=pltpu.SMEM)
    dma = pltpu.SemaphoreType.DMA
    block = (TILE, FEATS)
    flops = 2 * NODE_DEV * HIDDEN_SIZE * FEATS * 6 + 4 * slots * TILE * TILE * FEATS
    feat_grad, self_grad, neigh_grad, bias_grad = pl.pallas_call(
        functools.partial(kernel, n),
        out_shape=(
            jax.ShapeDtypeStruct((BLOCKS,) + block, BF16),
            jax.ShapeDtypeStruct((FEATS, width // 2), F32),
            jax.ShapeDtypeStruct((FEATS, width // 2), F32),
            jax.ShapeDtypeStruct((1, width // 2), F32),
        ),
        in_specs=[vmem, vmem, smem, smem, vmem, vmem, vmem, pl.BlockSpec(memory_space=pl.ANY)],
        out_specs=(vmem, vmem, vmem, vmem),
        scratch_shapes=[
            pltpu.VMEM((NODE_DEV, HIDDEN_SIZE), BF16),
            pltpu.VMEM((n, CAPACITY) + block, BF16),
            pltpu.VMEM((n, CAPACITY) + block, BF16),
            pltpu.VMEM((n, CAPACITY) + block, BF16),
            pltpu.VMEM((n, CAPACITY) + block, BF16),
            pltpu.VMEM((slots + 1,) + block, F32),
            pltpu.VMEM((2 * FEATS, HIDDEN_SIZE), BF16),
            pltpu.VMEM((NODE_DEV, 2 * FEATS), BF16),
            pltpu.VMEM((ROWS, HIDDEN_SIZE), F32),
            pltpu.VMEM((NODE_DEV, HIDDEN_SIZE), BF16),
            pltpu.VMEM((BLOCKS,) + block, BF16),
            pltpu.VMEM((BLOCKS,) + block, F32),
            pltpu.VMEM((2, FEATS, HIDDEN_SIZE), F32),
            pltpu.VMEM((8, HIDDEN_SIZE), F32),
            pltpu.VMEM((chips, share_rows, width), BF16),
            pltpu.VMEM((chips, share_rows, width), BF16),
            pltpu.VMEM((chips, share_rows, width), BF16),
            pltpu.VMEM((chips, share_rows, width), BF16),
            pltpu.VMEM((share_rows, width), F32),
            pltpu.VMEM((share_rows, width), F32),
            pltpu.SMEM((slots,), jnp.int32),
            pltpu.SMEM((BLOCKS + 1,), jnp.int32),
            pltpu.SMEM((slots,), jnp.int32),
            pltpu.SMEM((BLOCKS + 1,), jnp.int32),
            dma,
            dma((n,)),
            dma((n,)),
            dma((n,)),
            dma((n,)),
            dma((2,)),
            dma((chips,)),
            dma((chips,)),
            dma((2,)),
        ],
        compiler_params=pltpu.CompilerParams(
            collective_id=0, has_side_effects=True, vmem_limit_bytes=56 * 2**20
        ),
        cost_estimate=pl.CostEstimate(flops=flops, bytes_accessed=8 * 2**20, transcendentals=0),
    )(
        node_feats.reshape((BLOCKS,) + block),
        tile_weights,
        source_slots,
        target_slots,
        self_weight,
        neigh_weight,
        hidden_bias.reshape(1, HIDDEN_SIZE),
        out_grad,
    )
    return (
        feat_grad.reshape(NODE_DEV, FEATS),
        self_grad,
        neigh_grad,
        bias_grad.reshape(width // 2),
    )


def solution(mesh):
    in_specs = (
        P(("grp", "feat"), None),
        P(("grp", "feat"), None, None),
        P(("grp", "feat")),
        P(("grp", "feat")),
        P(),
        P(),
        P(),
        P(("grp", "feat"), None),
    )
    out_specs = (P(("grp", "feat"), None), P("grp", "feat"), P("grp", "feat"), P(("grp", "feat")))
    return jax.shard_map(local, mesh=mesh, in_specs=in_specs, out_specs=out_specs, check_vma=False)
```

```python
import functools

import jax
import jax.numpy as jnp
from jax import lax
from jax.experimental import pallas as pl
from jax.experimental.pallas import tpu as pltpu
from jax.sharding import PartitionSpec as P

FEATS = 128
HIDDEN_SIZE = 1024
TILE = 128
CAPACITY = 2
NODE_DEV = 2048
BLOCKS = NODE_DEV // TILE
ROWS = 256
COLS = 256
BIAS_ROWS = 16
EARLY = 3
PARTS = 2
SLAB = TILE // PARTS
PART_ROWS = NODE_DEV // PARTS
MESH = pl.DeviceIdType.MESH
F32 = jnp.float32
BF16 = jnp.bfloat16


def distance(step, n):
    q = jnp.maximum(step - 1, 0)
    far = n // 2 + ((q + 1) // 2) * (1 - 2 * (q % 2))
    return far * jnp.minimum(step, 1)


def split_bias(total):
    high = total.astype(BF16)
    low = (total - high.astype(F32)).astype(BF16)
    row = lax.broadcasted_iota(jnp.int32, (BIAS_ROWS, total.shape[1]), 0)
    both = jnp.where(row == 0, high.astype(F32), jnp.where(row == 1, low.astype(F32), 0.0))
    return both.astype(BF16)


def kernel(
    n,
    feats,
    tiles,
    source,
    target,
    self_w,
    neigh_w,
    bias,
    grad_hbm,
    feat_out,
    self_out,
    neigh_out,
    bias_out,
    grad,
    stage,
    arrived,
    back_stage,
    back,
    chain,
    weights,
    inputs,
    active,
    pre_grad,
    mean_grad,
    feat_self,
    weight_sum,
    bias_sum,
    pair_send,
    pair_recv,
    share_send,
    share_recv,
    swap_send,
    swap_recv,
    prev_t,
    last_t,
    prev_s,
    last_s,
    grad_sem,
    send_1,
    recv_1,
    send_2,
    recv_2,
    pair_sems,
    send_b,
    recv_b,
    swap_sems,
):
    chips = n // 2
    width = 2 * HIDDEN_SIZE // n
    half = width // 2
    slots = n * CAPACITY
    me = lax.axis_index("feat")
    core = me % 2
    chip = me // 2
    sibling = chip * 2 + 1 - core

    barrier = pltpu.get_barrier_semaphore()

    @pl.loop(1, n)
    def _(d):
        pl.semaphore_signal(
            barrier, inc=1, device_id={"feat": (me + d) % n}, device_id_type=MESH
        )

    grad_copies = [
        pltpu.make_async_copy(grad_hbm.at[:, h], grad.at[h], grad_sem.at[h]) for h in range(PARTS)
    ]
    for copy in grad_copies:
        copy.start()

    def slab(h):
        return slice(h * SLAB, (h + 1) * SLAB)

    def product(slot):
        block = feats[jnp.minimum(source[slot], BLOCKS - 1)]
        return jnp.dot(tiles[slot], block, preferred_element_type=F32).astype(BF16)

    def forward_copy(step, h):
        to = (me + distance(step, n)) % n
        return pltpu.make_async_remote_copy(
            src_ref=stage.at[to, :, slab(h)],
            dst_ref=arrived.at[me, :, slab(h)],
            send_sem=send_1.at[h, to],
            recv_sem=recv_1.at[h, me],
            device_id={"feat": to},
            device_id_type=MESH,
        )

    def forward_products(step):
        to = (me + distance(step, n)) % n
        for k in range(CAPACITY):
            stage[to, k] = product(to * CAPACITY + k)

    @pl.loop(1, 1 + EARLY)
    def _(step):
        forward_products(step)

    pl.semaphore_wait(barrier, n - 1)

    @pl.loop(1, 1 + EARLY)
    def _(step):
        forward_copy(step, 0).start()

    @pl.loop(1 + EARLY, n)
    def _(step):
        forward_products(step)
        forward_copy(step, 0).start()

    for h in range(1, PARTS):

        @pl.loop(1, n)
        def _(step):
            forward_copy(step, h).start()

    def rows_of(h, b):
        start = h * PART_ROWS + b * SLAB
        return slice(start, start + SLAB)

    for k in range(CAPACITY):
        arrived[me, k] = product(me * CAPACITY + k)
    weights[:FEATS] = self_w[...]
    weights[FEATS:] = neigh_w[...]
    for h in range(PARTS):
        for b in range(BLOCKS):
            inputs[rows_of(h, b), :FEATS] = feats[b, slab(h)]
    chain[slots] = jnp.zeros((TILE, FEATS), F32)
    bias_sum[...] = jnp.zeros_like(bias_sum)

    for prev, last, table in ((prev_t, last_t, target), (prev_s, last_s, source)):
        for b in range(BLOCKS + 1):
            last[b] = slots

        @pl.loop(0, n)
        def _(step):
            owner = (me - distance(step, n) + n) % n
            for k in range(CAPACITY):
                at = step * CAPACITY + k
                block = table[owner * CAPACITY + k]
                prev[at] = last[block]
                for b in range(BLOCKS + 1):
                    last[b] = jnp.where(block == b, at, last[b])

    def forward_link(h, step, owner):
        for k in range(CAPACITY):
            at = step * CAPACITY + k
            chain[at, slab(h)] = arrived[owner, k, slab(h)].astype(F32) + chain[prev_t[at], slab(h)]

    def take_forward(h):
        forward_link(h, 0, me)

        @pl.loop(1, n)
        def _(step):
            owner = (me - distance(step, n) + n) % n
            pltpu.make_async_remote_copy(
                src_ref=stage.at[owner, :, slab(h)],
                dst_ref=arrived.at[owner, :, slab(h)],
                send_sem=send_1.at[h, owner],
                recv_sem=recv_1.at[h, owner],
                device_id={"feat": owner},
                device_id_type=MESH,
            ).wait_recv()
            forward_link(h, step, owner)

        for b in range(BLOCKS):
            inputs[rows_of(h, b), FEATS:] = chain[last_t[b], slab(h)].astype(BF16)

    def layer(h):
        grad_copies[h].wait()
        group = ROWS // SLAB

        @pl.loop(0, PART_ROWS // ROWS)
        def _(part):
            rows = pl.ds(pl.multiple_of(h * PART_ROWS + part * ROWS, ROWS), ROWS)
            blocks = pl.ds(part * group, group)
            x = inputs[rows, :]
            squares = jnp.zeros((ROWS, 128), F32)
            crosses = jnp.zeros((ROWS, 128), F32)
            for c in range(0, HIDDEN_SIZE, COLS):
                cols = slice(c, c + COLS)
                pre = jnp.dot(x, weights[:, cols], preferred_element_type=F32) + bias[:, cols]
                a = jnp.maximum(pre, 0.0)
                active[:, cols] = a
                g = grad[h, blocks, :, cols].reshape(ROWS, COLS).astype(F32)
                aa = a * a
                ag = a * g
                for e in range(0, COLS, 128):
                    squares += aa[:, e : e + 128]
                    crosses += ag[:, e : e + 128]
            scale = lax.rsqrt(jnp.sum(squares, axis=1, keepdims=True) / HIDDEN_SIZE + 1e-05)
            pull = scale * scale * scale * (jnp.sum(crosses, axis=1, keepdims=True) / HIDDEN_SIZE)
            for c in range(0, HIDDEN_SIZE, COLS):
                cols = slice(c, c + COLS)
                a = active[:, cols]
                g = grad[h, blocks, :, cols].reshape(ROWS, COLS).astype(F32)
                p = jnp.where(a > 0.0, scale * g - pull * a, 0.0).astype(BF16)
                pre_grad[rows, cols] = p
                bias_sum[:, cols] += jnp.sum(p.astype(F32).reshape(ROWS // 8, 8, COLS), axis=0)
            both = lax.dot_general(
                pre_grad[rows, :],
                weights[...],
                (((1,), (1,)), ((), ())),
                preferred_element_type=F32,
            )
            for e in range(group):
                b = part * group + e
                feat_self[b, slab(h)] = both[e * SLAB : (e + 1) * SLAB, :FEATS]
                mean_grad[b, slab(h)] = both[e * SLAB : (e + 1) * SLAB, FEATS:].astype(BF16)

    def backward_copy(step, h):
        to = (me + distance(step, n)) % n
        return pltpu.make_async_remote_copy(
            src_ref=back_stage.at[to, :, slab(h)],
            dst_ref=back.at[me, :, slab(h)],
            send_sem=send_2.at[h, to],
            recv_sem=recv_2.at[h, me],
            device_id={"feat": to},
            device_id_type=MESH,
        )

    def backward_send(step, h):
        to = (me + distance(step, n)) % n
        for k in range(CAPACITY):
            block = jnp.minimum(target[to * CAPACITY + k], BLOCKS - 1)
            back_stage[to, k, slab(h)] = mean_grad[block, slab(h)]
        backward_copy(step, h).start()

    def weight_gradients(h):
        rows = slice(h * PART_ROWS, (h + 1) * PART_ROWS)
        for c in range(0, HIDDEN_SIZE, COLS):
            cols = slice(c, c + COLS)
            local = lax.dot_general(
                inputs[rows, :],
                pre_grad[rows, cols],
                (((0,), (0,)), ((), ())),
                preferred_element_type=F32,
            )
            if h == 0:
                weight_sum[0, :, cols] = local[:FEATS]
                weight_sum[1, :, cols] = local[FEATS:]
            else:
                weight_sum[0, :, cols] += local[:FEATS]
                weight_sum[1, :, cols] += local[FEATS:]

    for h in range(PARTS):
        take_forward(h)
        layer(h)

        @pl.loop(1, 1 + n // 2 if h == PARTS - 1 else n)
        def _(step):
            backward_send(step, h)

        weight_gradients(h)

    bias_row = jnp.sum(bias_sum[...], axis=0, keepdims=True)
    for c in range(chips):
        cols = slice(c * width, (c + 1) * width)
        pair_send[c, :FEATS] = weight_sum[1 - core, :, cols].astype(BF16)
        pair_send[c, FEATS:] = split_bias(bias_row[:, cols])
    pair_copy = pltpu.make_async_remote_copy(
        src_ref=pair_send,
        dst_ref=pair_recv,
        send_sem=pair_sems.at[0],
        recv_sem=pair_sems.at[1],
        device_id={"feat": sibling},
        device_id_type=MESH,
    )
    pair_copy.start()
    pair_copy.wait_recv()
    for c in range(chips):
        cols = slice(c * width, (c + 1) * width)
        share_send[c, :FEATS] = (
            weight_sum[core, :, cols] + pair_recv[c, :FEATS].astype(F32)
        ).astype(BF16)
        other = jnp.sum(pair_recv[c, FEATS:].astype(F32), axis=0, keepdims=True)
        share_send[c, FEATS:] = split_bias(bias_row[:, cols] + other)

    def share_copy(to, slot):
        return pltpu.make_async_remote_copy(
            src_ref=share_send.at[to],
            dst_ref=share_recv.at[slot],
            send_sem=send_b.at[to],
            recv_sem=recv_b.at[slot],
            device_id={"feat": to * 2 + core},
            device_id_type=MESH,
        )

    @pl.loop(1, chips)
    def _(d):
        share_copy((chip + d) % chips, chip).start()

    @pl.loop(1 + n // 2, n)
    def _(step):
        backward_send(step, PARTS - 1)

    def backward_link(step, owner, blocks):
        for k in range(CAPACITY):
            at = step * CAPACITY + k
            spread = lax.dot_general(
                tiles[owner * CAPACITY + k],
                blocks[k],
                (((0,), (0,)), ((), ())),
                preferred_element_type=F32,
            )
            chain[at] = spread + chain[prev_s[at]]

    backward_link(
        0,
        me,
        [
            mean_grad[jnp.minimum(target[me * CAPACITY + k], BLOCKS - 1)]
            for k in range(CAPACITY)
        ],
    )

    def backward_take(step):
        owner = (me - distance(step, n) + n) % n
        for h in range(PARTS):
            pltpu.make_async_remote_copy(
                src_ref=back_stage.at[owner, :, slab(h)],
                dst_ref=back.at[owner, :, slab(h)],
                send_sem=send_2.at[h, owner],
                recv_sem=recv_2.at[h, owner],
                device_id={"feat": owner},
                device_id_type=MESH,
            ).wait_recv()
        backward_link(step, owner, [back[owner, k] for k in range(CAPACITY)])

    @pl.loop(1, 1 + n // 2)
    def _(step):
        backward_take(step)

    swap_send[...] = share_send[chip].astype(F32)

    @pl.loop(1, chips)
    def _(d):
        other = (chip + d) % chips
        share_copy(other, other).wait_recv()
        swap_send[...] += share_recv[other].astype(F32)

    swap_copy = pltpu.make_async_remote_copy(
        src_ref=swap_send,
        dst_ref=swap_recv,
        send_sem=swap_sems.at[0],
        recv_sem=swap_sems.at[1],
        device_id={"feat": sibling},
        device_id_type=MESH,
    )
    swap_copy.start()

    @pl.loop(1 + n // 2, n)
    def _(step):
        backward_take(step)

    for b in range(BLOCKS):
        feat_out[b] = (feat_self[b] + chain[last_s[b]]).astype(BF16)

    swap_copy.wait_recv()

    def own_half(block):
        return jnp.where(core == 0, block[:, :half], block[:, half:])

    mine = own_half(swap_send[:FEATS])
    theirs = own_half(swap_recv[:FEATS])
    self_out[...] = jnp.where(core == 0, mine, theirs).T
    neigh_out[...] = jnp.where(core == 0, theirs, mine).T
    bias_out[...] = own_half(jnp.sum(swap_send[FEATS:], axis=0, keepdims=True))

    swap_copy.wait_send()
    pair_copy.wait_send()

    @pl.loop(1, chips)
    def _(d):
        share_copy((chip + d) % chips, chip).wait_send()

    @pl.loop(1, n)
    def _(step):
        for h in range(PARTS):
            forward_copy(step, h).wait_send()
            backward_copy(step, h).wait_send()


def hand_on(*refs):
    for i in range(4):
        refs[4 + i][...] = refs[i][...]


def local(
    node_feats,
    tile_weights,
    source_slots,
    target_slots,
    self_weight,
    neigh_weight,
    hidden_bias,
    out_grad,
):
    n = lax.axis_size("feat")
    slots = n * CAPACITY
    chips = n // 2
    width = 2 * HIDDEN_SIZE // n
    share_rows = FEATS + BIAS_ROWS
    vmem = pl.BlockSpec(memory_space=pltpu.VMEM)
    smem = pl.BlockSpec(memory_space=pltpu.SMEM)
    dma = pltpu.SemaphoreType.DMA
    block = (TILE, FEATS)
    flops = 2 * NODE_DEV * HIDDEN_SIZE * FEATS * 6 + 4 * slots * TILE * TILE * FEATS
    feat_grad, self_grad, neigh_grad, bias_grad = pl.pallas_call(
        functools.partial(kernel, n),
        out_shape=(
            jax.ShapeDtypeStruct((BLOCKS,) + block, BF16),
            jax.ShapeDtypeStruct((width // 2, FEATS), F32),
            jax.ShapeDtypeStruct((width // 2, FEATS), F32),
            jax.ShapeDtypeStruct((1, width // 2), F32),
        ),
        in_specs=[vmem, vmem, smem, smem, vmem, vmem, vmem, pl.BlockSpec(memory_space=pl.ANY)],
        out_specs=(vmem, vmem, vmem, vmem),
        scratch_shapes=[
            pltpu.VMEM((PARTS, BLOCKS, SLAB, HIDDEN_SIZE), BF16),
            pltpu.VMEM((n, CAPACITY) + block, BF16),
            pltpu.VMEM((n, CAPACITY) + block, BF16),
            pltpu.VMEM((n, CAPACITY) + block, BF16),
            pltpu.VMEM((n, CAPACITY) + block, BF16),
            pltpu.VMEM((slots + 1,) + block, F32),
            pltpu.VMEM((2 * FEATS, HIDDEN_SIZE), BF16),
            pltpu.VMEM((NODE_DEV, 2 * FEATS), BF16),
            pltpu.VMEM((ROWS, HIDDEN_SIZE), F32),
            pltpu.VMEM((NODE_DEV, HIDDEN_SIZE), BF16),
            pltpu.VMEM((BLOCKS,) + block, BF16),
            pltpu.VMEM((BLOCKS,) + block, F32),
            pltpu.VMEM((2, FEATS, HIDDEN_SIZE), F32),
            pltpu.VMEM((8, HIDDEN_SIZE), F32),
            pltpu.VMEM((chips, share_rows, width), BF16),
            pltpu.VMEM((chips, share_rows, width), BF16),
            pltpu.VMEM((chips, share_rows, width), BF16),
            pltpu.VMEM((chips, share_rows, width), BF16),
            pltpu.VMEM((share_rows, width), F32),
            pltpu.VMEM((share_rows, width), F32),
            pltpu.SMEM((slots,), jnp.int32),
            pltpu.SMEM((BLOCKS + 1,), jnp.int32),
            pltpu.SMEM((slots,), jnp.int32),
            pltpu.SMEM((BLOCKS + 1,), jnp.int32),
            dma((PARTS,)),
            dma((PARTS, n)),
            dma((PARTS, n)),
            dma((PARTS, n)),
            dma((PARTS, n)),
            dma((2,)),
            dma((chips,)),
            dma((chips,)),
            dma((2,)),
        ],
        compiler_params=pltpu.CompilerParams(
            collective_id=0, has_side_effects=True, vmem_limit_bytes=56 * 2**20
        ),
        cost_estimate=pl.CostEstimate(flops=flops, bytes_accessed=8 * 2**20, transcendentals=0),
    )(
        node_feats.reshape((BLOCKS,) + block),
        tile_weights,
        source_slots,
        target_slots,
        self_weight,
        neigh_weight,
        hidden_bias.reshape(1, HIDDEN_SIZE),
        out_grad.reshape(BLOCKS, PARTS, SLAB, HIDDEN_SIZE),
    )
    results = (feat_grad, self_grad, neigh_grad, bias_grad)
    feat_grad, self_grad, neigh_grad, bias_grad = pl.pallas_call(
        hand_on,
        out_shape=tuple(jax.ShapeDtypeStruct(r.shape, r.dtype) for r in results),
        in_specs=[vmem] * 4,
        out_specs=(vmem,) * 4,
        cost_estimate=pl.CostEstimate(flops=0, bytes_accessed=2**20, transcendentals=0),
    )(*results)
    return (
        feat_grad.reshape(NODE_DEV, FEATS),
        self_grad.T,
        neigh_grad.T,
        bias_grad.reshape(width // 2),
    )


def solution(mesh):
    in_specs = (
        P(("grp", "feat"), None),
        P(("grp", "feat"), None, None),
        P(("grp", "feat")),
        P(("grp", "feat")),
        P(),
        P(),
        P(),
        P(("grp", "feat"), None),
    )
    out_specs = (P(("grp", "feat"), None), P("grp", "feat"), P("grp", "feat"), P(("grp", "feat")))
    return jax.shard_map(local, mesh=mesh, in_specs=in_specs, out_specs=out_specs, check_vma=False)
```

```python
import functools

import jax
import jax.numpy as jnp
from jax import lax
from jax.experimental import pallas as pl
from jax.experimental.pallas import tpu as pltpu
from jax.sharding import PartitionSpec as P

FEATS = 128
HIDDEN_SIZE = 1024
TILE = 128
CAPACITY = 2
NODE_DEV = 2048
BLOCKS = NODE_DEV // TILE
ROWS = 256
COLS = 256
BIAS_ROWS = 16
EARLY = 3
PARTS = 2
AHEAD = (4, 5, 6)
SLAB = TILE // PARTS
PART_ROWS = NODE_DEV // PARTS
MESH = pl.DeviceIdType.MESH
F32 = jnp.float32
BF16 = jnp.bfloat16


def distance(step, n):
    q = jnp.maximum(step - 1, 0)
    far = n // 2 + ((q + 1) // 2) * (1 - 2 * (q % 2))
    return far * jnp.minimum(step, 1)


def split_bias(total):
    high = total.astype(BF16)
    low = (total - high.astype(F32)).astype(BF16)
    row = lax.broadcasted_iota(jnp.int32, (BIAS_ROWS, total.shape[1]), 0)
    both = jnp.where(row == 0, high.astype(F32), jnp.where(row == 1, low.astype(F32), 0.0))
    return both.astype(BF16)


def kernel(
    n,
    feats,
    tiles,
    source,
    target,
    self_w,
    neigh_w,
    bias,
    grad_hbm,
    feat_out,
    self_out,
    neigh_out,
    bias_out,
    grad,
    stage,
    arrived,
    back_stage,
    back,
    chain,
    weights,
    inputs,
    active,
    pre_grad,
    mean_grad,
    feat_self,
    weight_sum,
    bias_sum,
    pair_send,
    pair_recv,
    share_send,
    side_recv,
    layer_send,
    share_recv,
    swap_send,
    swap_recv,
    prev_t,
    last_t,
    prev_s,
    last_s,
    grad_sem,
    send_1,
    recv_1,
    send_2,
    recv_2,
    pair_sems,
    side_sems,
    send_b,
    recv_b,
    swap_sems,
):
    chips = n // 2
    width = 2 * HIDDEN_SIZE // n
    half = width // 2
    slots = n * CAPACITY
    me = lax.axis_index("feat")
    core = me % 2
    chip = me // 2
    sibling = chip * 2 + 1 - core
    layers = chips // 2
    side = chip % 2
    layer_id = chip // 2
    beside = (layer_id * 2 + 1 - side) * 2 + core

    barrier = pltpu.get_barrier_semaphore()

    @pl.loop(1, n)
    def _(d):
        pl.semaphore_signal(
            barrier, inc=1, device_id={"feat": (me + d) % n}, device_id_type=MESH
        )

    grad_copies = [
        pltpu.make_async_copy(grad_hbm.at[:, h], grad.at[h], grad_sem.at[h]) for h in range(PARTS)
    ]
    for copy in grad_copies:
        copy.start()

    def slab(h):
        return slice(h * SLAB, (h + 1) * SLAB)

    def product(slot):
        block = feats[jnp.minimum(source[slot], BLOCKS - 1)]
        return jnp.dot(tiles[slot], block, preferred_element_type=F32).astype(BF16)

    def forward_copy(step, h):
        to = (me + distance(step, n)) % n
        return pltpu.make_async_remote_copy(
            src_ref=stage.at[to, :, slab(h)],
            dst_ref=arrived.at[me, :, slab(h)],
            send_sem=send_1.at[h, to],
            recv_sem=recv_1.at[h, me],
            device_id={"feat": to},
            device_id_type=MESH,
        )

    def forward_products(step):
        to = (me + distance(step, n)) % n
        for k in range(CAPACITY):
            stage[to, k] = product(to * CAPACITY + k)

    @pl.loop(1, 1 + EARLY)
    def _(step):
        forward_products(step)

    pl.semaphore_wait(barrier, n - 1)

    @pl.loop(1, 1 + EARLY)
    def _(step):
        forward_copy(step, 0).start()

    @pl.loop(1 + EARLY, n)
    def _(step):
        forward_products(step)
        forward_copy(step, 0).start()

    for h in range(1, PARTS):

        @pl.loop(1, n)
        def _(step):
            forward_copy(step, h).start()

    def rows_of(h, b):
        start = h * PART_ROWS + b * SLAB
        return slice(start, start + SLAB)

    for k in range(CAPACITY):
        arrived[me, k] = product(me * CAPACITY + k)
    weights[:FEATS] = self_w[...]
    weights[FEATS:] = neigh_w[...]
    for h in range(PARTS):
        for b in range(BLOCKS):
            inputs[rows_of(h, b), :FEATS] = feats[b, slab(h)]
    chain[slots] = jnp.zeros((TILE, FEATS), F32)
    bias_sum[...] = jnp.zeros_like(bias_sum)

    for prev, last, table in ((prev_t, last_t, target), (prev_s, last_s, source)):
        for b in range(BLOCKS + 1):
            last[b] = slots

        @pl.loop(0, n)
        def _(step):
            owner = (me - distance(step, n) + n) % n
            for k in range(CAPACITY):
                at = step * CAPACITY + k
                block = table[owner * CAPACITY + k]
                prev[at] = last[block]
                for b in range(BLOCKS + 1):
                    last[b] = jnp.where(block == b, at, last[b])

    def forward_link(h, step, owner):
        for k in range(CAPACITY):
            at = step * CAPACITY + k
            chain[at, slab(h)] = arrived[owner, k, slab(h)].astype(F32) + chain[prev_t[at], slab(h)]

    def take_forward(h):
        forward_link(h, 0, me)

        @pl.loop(1, n)
        def _(step):
            owner = (me - distance(step, n) + n) % n
            pltpu.make_async_remote_copy(
                src_ref=stage.at[owner, :, slab(h)],
                dst_ref=arrived.at[owner, :, slab(h)],
                send_sem=send_1.at[h, owner],
                recv_sem=recv_1.at[h, owner],
                device_id={"feat": owner},
                device_id_type=MESH,
            ).wait_recv()
            forward_link(h, step, owner)

        for b in range(BLOCKS):
            inputs[rows_of(h, b), FEATS:] = chain[last_t[b], slab(h)].astype(BF16)

    def layer(h):
        grad_copies[h].wait()
        group = ROWS // SLAB

        @pl.loop(0, PART_ROWS // ROWS)
        def _(part):
            rows = pl.ds(pl.multiple_of(h * PART_ROWS + part * ROWS, ROWS), ROWS)
            blocks = pl.ds(part * group, group)
            x = inputs[rows, :]
            squares = jnp.zeros((ROWS, 128), F32)
            crosses = jnp.zeros((ROWS, 128), F32)
            for c in range(0, HIDDEN_SIZE, COLS):
                cols = slice(c, c + COLS)
                pre = jnp.dot(x, weights[:, cols], preferred_element_type=F32) + bias[:, cols]
                a = jnp.maximum(pre, 0.0)
                active[:, cols] = a
                g = grad[h, blocks, :, cols].reshape(ROWS, COLS).astype(F32)
                aa = a * a
                ag = a * g
                for e in range(0, COLS, 128):
                    squares += aa[:, e : e + 128]
                    crosses += ag[:, e : e + 128]
            scale = lax.rsqrt(jnp.sum(squares, axis=1, keepdims=True) / HIDDEN_SIZE + 1e-05)
            pull = scale * scale * scale * (jnp.sum(crosses, axis=1, keepdims=True) / HIDDEN_SIZE)
            for c in range(0, HIDDEN_SIZE, COLS):
                cols = slice(c, c + COLS)
                a = active[:, cols]
                g = grad[h, blocks, :, cols].reshape(ROWS, COLS).astype(F32)
                p = jnp.where(a > 0.0, scale * g - pull * a, 0.0).astype(BF16)
                pre_grad[rows, cols] = p
                bias_sum[:, cols] += jnp.sum(p.astype(F32).reshape(ROWS // 8, 8, COLS), axis=0)
            both = lax.dot_general(
                pre_grad[rows, :],
                weights[...],
                (((1,), (1,)), ((), ())),
                preferred_element_type=F32,
            )
            for e in range(group):
                b = part * group + e
                feat_self[b, slab(h)] = both[e * SLAB : (e + 1) * SLAB, :FEATS]
                mean_grad[b, slab(h)] = both[e * SLAB : (e + 1) * SLAB, FEATS:].astype(BF16)

    def backward_copy(step, h):
        to = (me + distance(step, n)) % n
        return pltpu.make_async_remote_copy(
            src_ref=back_stage.at[to, :, slab(h)],
            dst_ref=back.at[me, :, slab(h)],
            send_sem=send_2.at[h, to],
            recv_sem=recv_2.at[h, me],
            device_id={"feat": to},
            device_id_type=MESH,
        )

    def backward_send(step, h):
        to = (me + distance(step, n)) % n
        for k in range(CAPACITY):
            block = jnp.minimum(target[to * CAPACITY + k], BLOCKS - 1)
            back_stage[to, k, slab(h)] = mean_grad[block, slab(h)]
        backward_copy(step, h).start()

    def last_sends(first, end):
        @pl.loop(first, end)
        def _(step):
            backward_send(step, PARTS - 1)

    def weight_gradients(h):
        rows = slice(h * PART_ROWS, (h + 1) * PART_ROWS)
        for c in range(0, HIDDEN_SIZE, COLS):
            cols = slice(c, c + COLS)
            local = lax.dot_general(
                inputs[rows, :],
                pre_grad[rows, cols],
                (((0,), (0,)), ((), ())),
                preferred_element_type=F32,
            )
            if h == 0:
                weight_sum[0, :, cols] = local[:FEATS]
                weight_sum[1, :, cols] = local[FEATS:]
            else:
                weight_sum[0, :, cols] += local[:FEATS]
                weight_sum[1, :, cols] += local[FEATS:]

    for h in range(PARTS):
        take_forward(h)
        layer(h)

        @pl.loop(1, 1 + n * AHEAD[0] // 8 if h == PARTS - 1 else n)
        def _(step):
            backward_send(step, h)

        weight_gradients(h)

    bias_row = jnp.sum(bias_sum[...], axis=0, keepdims=True)
    for c in range(chips):
        cols = slice(c * width, (c + 1) * width)
        pair_send[c, :FEATS] = weight_sum[1 - core, :, cols].astype(BF16)
        pair_send[c, FEATS:] = split_bias(bias_row[:, cols])
    pair_copy = pltpu.make_async_remote_copy(
        src_ref=pair_send,
        dst_ref=pair_recv,
        send_sem=pair_sems.at[0],
        recv_sem=pair_sems.at[1],
        device_id={"feat": sibling},
        device_id_type=MESH,
    )
    pair_copy.start()
    last_sends(1 + n * AHEAD[0] // 8, 1 + n * AHEAD[1] // 8)
    pair_copy.wait_recv()
    for c in range(chips):
        cols = slice(c * width, (c + 1) * width)
        share_send[c % 2, c // 2, :FEATS] = (
            weight_sum[core, :, cols] + pair_recv[c, :FEATS].astype(F32)
        ).astype(BF16)
        other = jnp.sum(pair_recv[c, FEATS:].astype(F32), axis=0, keepdims=True)
        share_send[c % 2, c // 2, FEATS:] = split_bias(bias_row[:, cols] + other)

    side_copy = pltpu.make_async_remote_copy(
        src_ref=share_send.at[1 - side],
        dst_ref=side_recv,
        send_sem=side_sems.at[0],
        recv_sem=side_sems.at[1],
        device_id={"feat": beside},
        device_id_type=MESH,
    )
    side_copy.start()
    last_sends(1 + n * AHEAD[1] // 8, 1 + n * AHEAD[2] // 8)
    side_copy.wait_recv()
    for c in range(layers):
        summed = share_send[side, c].astype(F32) + side_recv[c].astype(F32)
        layer_send[c, :FEATS] = summed[:FEATS].astype(BF16)
        layer_send[c, FEATS:] = split_bias(jnp.sum(summed[FEATS:], axis=0, keepdims=True))

    def share_copy(to, slot):
        return pltpu.make_async_remote_copy(
            src_ref=layer_send.at[to],
            dst_ref=share_recv.at[slot],
            send_sem=send_b.at[to],
            recv_sem=recv_b.at[slot],
            device_id={"feat": (to * 2 + side) * 2 + core},
            device_id_type=MESH,
        )

    @pl.loop(1, layers)
    def _(d):
        share_copy((layer_id + d) % layers, layer_id).start()

    last_sends(1 + n * AHEAD[2] // 8, n)

    def backward_link(step, owner, blocks):
        for k in range(CAPACITY):
            at = step * CAPACITY + k
            spread = lax.dot_general(
                tiles[owner * CAPACITY + k],
                blocks[k],
                (((0,), (0,)), ((), ())),
                preferred_element_type=F32,
            )
            chain[at] = spread + chain[prev_s[at]]

    backward_link(
        0,
        me,
        [
            mean_grad[jnp.minimum(target[me * CAPACITY + k], BLOCKS - 1)]
            for k in range(CAPACITY)
        ],
    )

    def backward_take(step):
        owner = (me - distance(step, n) + n) % n
        for h in range(PARTS):
            pltpu.make_async_remote_copy(
                src_ref=back_stage.at[owner, :, slab(h)],
                dst_ref=back.at[owner, :, slab(h)],
                send_sem=send_2.at[h, owner],
                recv_sem=recv_2.at[h, owner],
                device_id={"feat": owner},
                device_id_type=MESH,
            ).wait_recv()
        backward_link(step, owner, [back[owner, k] for k in range(CAPACITY)])

    @pl.loop(1, 1 + n // 2)
    def _(step):
        backward_take(step)

    swap_send[...] = layer_send[layer_id].astype(F32)

    @pl.loop(1, layers)
    def _(d):
        other = (layer_id + d) % layers
        share_copy(other, other).wait_recv()
        swap_send[...] += share_recv[other].astype(F32)

    swap_copy = pltpu.make_async_remote_copy(
        src_ref=swap_send,
        dst_ref=swap_recv,
        send_sem=swap_sems.at[0],
        recv_sem=swap_sems.at[1],
        device_id={"feat": sibling},
        device_id_type=MESH,
    )
    swap_copy.start()

    @pl.loop(1 + n // 2, n)
    def _(step):
        backward_take(step)

    for b in range(BLOCKS):
        feat_out[b] = (feat_self[b] + chain[last_s[b]]).astype(BF16)

    swap_copy.wait_recv()

    def own_half(block):
        return jnp.where(core == 0, block[:, :half], block[:, half:])

    mine = own_half(swap_send[:FEATS])
    theirs = own_half(swap_recv[:FEATS])
    self_out[...] = jnp.where(core == 0, mine, theirs).T
    neigh_out[...] = jnp.where(core == 0, theirs, mine).T
    bias_out[...] = own_half(jnp.sum(swap_send[FEATS:], axis=0, keepdims=True))

    swap_copy.wait_send()
    pair_copy.wait_send()
    side_copy.wait_send()

    @pl.loop(1, layers)
    def _(d):
        share_copy((layer_id + d) % layers, layer_id).wait_send()

    @pl.loop(1, n)
    def _(step):
        for h in range(PARTS):
            forward_copy(step, h).wait_send()
            backward_copy(step, h).wait_send()


def hand_on(*refs):
    for i in range(4):
        refs[4 + i][...] = refs[i][...]


def local(
    node_feats,
    tile_weights,
    source_slots,
    target_slots,
    self_weight,
    neigh_weight,
    hidden_bias,
    out_grad,
):
    n = lax.axis_size("feat")
    slots = n * CAPACITY
    chips = n // 2
    width = 2 * HIDDEN_SIZE // n
    share_rows = FEATS + BIAS_ROWS
    vmem = pl.BlockSpec(memory_space=pltpu.VMEM)
    smem = pl.BlockSpec(memory_space=pltpu.SMEM)
    dma = pltpu.SemaphoreType.DMA
    block = (TILE, FEATS)
    flops = 2 * NODE_DEV * HIDDEN_SIZE * FEATS * 6 + 4 * slots * TILE * TILE * FEATS
    feat_grad, self_grad, neigh_grad, bias_grad = pl.pallas_call(
        functools.partial(kernel, n),
        out_shape=(
            jax.ShapeDtypeStruct((BLOCKS,) + block, BF16),
            jax.ShapeDtypeStruct((width // 2, FEATS), F32),
            jax.ShapeDtypeStruct((width // 2, FEATS), F32),
            jax.ShapeDtypeStruct((1, width // 2), F32),
        ),
        in_specs=[vmem, vmem, smem, smem, vmem, vmem, vmem, pl.BlockSpec(memory_space=pl.ANY)],
        out_specs=(vmem, vmem, vmem, vmem),
        scratch_shapes=[
            pltpu.VMEM((PARTS, BLOCKS, SLAB, HIDDEN_SIZE), BF16),
            pltpu.VMEM((n, CAPACITY) + block, BF16),
            pltpu.VMEM((n, CAPACITY) + block, BF16),
            pltpu.VMEM((n, CAPACITY) + block, BF16),
            pltpu.VMEM((n, CAPACITY) + block, BF16),
            pltpu.VMEM((slots + 1,) + block, F32),
            pltpu.VMEM((2 * FEATS, HIDDEN_SIZE), BF16),
            pltpu.VMEM((NODE_DEV, 2 * FEATS), BF16),
            pltpu.VMEM((ROWS, HIDDEN_SIZE), F32),
            pltpu.VMEM((NODE_DEV, HIDDEN_SIZE), BF16),
            pltpu.VMEM((BLOCKS,) + block, BF16),
            pltpu.VMEM((BLOCKS,) + block, F32),
            pltpu.VMEM((2, FEATS, HIDDEN_SIZE), F32),
            pltpu.VMEM((8, HIDDEN_SIZE), F32),
            pltpu.VMEM((chips, share_rows, width), BF16),
            pltpu.VMEM((chips, share_rows, width), BF16),
            pltpu.VMEM((2, chips // 2, share_rows, width), BF16),
            pltpu.VMEM((chips // 2, share_rows, width), BF16),
            pltpu.VMEM((chips // 2, share_rows, width), BF16),
            pltpu.VMEM((chips // 2, share_rows, width), BF16),
            pltpu.VMEM((share_rows, width), F32),
            pltpu.VMEM((share_rows, width), F32),
            pltpu.SMEM((slots,), jnp.int32),
            pltpu.SMEM((BLOCKS + 1,), jnp.int32),
            pltpu.SMEM((slots,), jnp.int32),
            pltpu.SMEM((BLOCKS + 1,), jnp.int32),
            dma((PARTS,)),
            dma((PARTS, n)),
            dma((PARTS, n)),
            dma((PARTS, n)),
            dma((PARTS, n)),
            dma((2,)),
            dma((2,)),
            dma((chips // 2,)),
            dma((chips // 2,)),
            dma((2,)),
        ],
        compiler_params=pltpu.CompilerParams(
            collective_id=0, has_side_effects=True, vmem_limit_bytes=56 * 2**20
        ),
        cost_estimate=pl.CostEstimate(flops=flops, bytes_accessed=8 * 2**20, transcendentals=0),
    )(
        node_feats.reshape((BLOCKS,) + block),
        tile_weights,
        source_slots,
        target_slots,
        self_weight,
        neigh_weight,
        hidden_bias.reshape(1, HIDDEN_SIZE),
        out_grad.reshape(BLOCKS, PARTS, SLAB, HIDDEN_SIZE),
    )
    results = (feat_grad, self_grad, neigh_grad, bias_grad)
    feat_grad, self_grad, neigh_grad, bias_grad = pl.pallas_call(
        hand_on,
        out_shape=tuple(jax.ShapeDtypeStruct(r.shape, r.dtype) for r in results),
        in_specs=[vmem] * 4,
        out_specs=(vmem,) * 4,
        cost_estimate=pl.CostEstimate(flops=0, bytes_accessed=2**20, transcendentals=0),
    )(*results)
    return (
        feat_grad.reshape(NODE_DEV, FEATS),
        self_grad.T,
        neigh_grad.T,
        bias_grad.reshape(width // 2),
    )


def solution(mesh):
    in_specs = (
        P(("grp", "feat"), None),
        P(("grp", "feat"), None, None),
        P(("grp", "feat")),
        P(("grp", "feat")),
        P(),
        P(),
        P(),
        P(("grp", "feat"), None),
    )
    out_specs = (P(("grp", "feat"), None), P("grp", "feat"), P("grp", "feat"), P(("grp", "feat")))
    return jax.shard_map(local, mesh=mesh, in_specs=in_specs, out_specs=out_specs, check_vma=False)
```
